512 devices in a mesh: row: 32 (over z, x), col: 16 (over y, core).
Axes of the slice: x: 4, y: 8, z: 8, core: 2. Of those that a mesh axis runs over, the one named last changes fastest.
Arguments:
- kernel: float32 [4, 4096, 8, 2048], P(None, 'row', None, 'col'), as said below
- targets: float32 [4, 32, 128, 1024], P(None, 'row', 'col'), may hold values from -6 to 6
Outputs:
- factor: float32 [4, 4096, 512], P(None, 'row')
- trailing: float32 [4, 4096, 8, 2048], P(None, 'row', None, 'col')
- targets_out: float32 [4, 32, 128, 1024], P(None, 'row', 'col')
The draws below stay inside these ranges and needn't reach their ends.
Inputs may be any that keep to these rules, and one draw needn't show every extreme that they name: kernel is symmetric and positive definite.
All inputs are finite; a program needn't handle non-finite values.
Results may differ from the reference program's by a relative error of at most 0.00018.
Values sent between devices are 32-bit elements; how exact they have to be, the bound alone decides.
No kernel may reach another device: no remote copies, remote signals or barrier semaphores. Data moves between devices by JAX's collectives and lax.ppermute only.
A program may use at most 64 MiB of HBM per device.

```python
import jax
import jax.numpy as jnp
from jax import lax

TB = 128
LR = 4
E = 1024
LC = 8
ORDER = 16384
N_ROW = 32
N_COL = 16


def similarity(positions, strength, spread):
    gap = (positions[:, None] - positions[None, :]) / spread
    return strength * jnp.exp(-(gap * gap))


def draw_kernel(key, part):
    key = jax.random.fold_in(key, 7)
    first, second, third = jax.random.split(key, 3)
    count = ORDER
    noise = jax.random.normal(first, (count, count), jnp.float32)
    diagonal = 4.0 + 3.0 * jax.random.uniform(second, (count,), jnp.float32)
    positions = jax.random.uniform(third, (count,), jnp.float32)
    smooth = similarity(positions, 0.25, 0.3)
    lower_part = jnp.tril(noise, -1)
    symmetric = (lower_part + lower_part.T) * (1.5 / count ** 0.5)
    matrix = symmetric + smooth + jnp.diag(diagonal)
    return matrix.reshape(LR, N_ROW * TB, LC, N_COL * TB)


def block_scale(rng, extent, cuts, smallest, high):
    factor_of, own = 1.0, jax.random.fold_in(rng, 6)
    for dim, blocks in cuts:
        draws = jnp.exp(jax.random.uniform(jax.random.fold_in(own, dim), (blocks,), jnp.float32, smallest / len(cuts), high / len(cuts)))
        factor_of = factor_of * jnp.repeat(draws, extent[dim] // blocks).reshape([-1 if axis == dim else 1 for axis in range(len(extent))])
    return factor_of


def centred(key, extent, scale, limit, shards=(), kind=jnp.bfloat16):
    values = jax.random.normal(key, extent, jnp.float32) * scale
    if len(shards) > 0:
        values = block_scale(key, extent, shards, -0.22, 0.18) * values
    return jnp.clip(values, min=-limit, max=limit).astype(kind)


def setup_inputs(seed: int = 0) -> dict:
    key_of = jax.random.split(jax.random.key(seed), 3)
    return {
        "kernel": draw_kernel(jax.random.fold_in(key_of[2], 71), 0),
        "targets": centred(key_of[1], (LR, N_ROW, TB, E), 1.0, 6.0, ((1, 32), (2, 16)), jnp.float32),
    }


def reference(kernel, targets):
    order = kernel.shape[0] * kernel.shape[1]
    width = 2 * TB
    matrix = kernel.reshape(order, order)
    wanted = targets.reshape(order, targets.shape[3])
    panels = []
    for k in range(2):
        start = k * width
        lower = jnp.linalg.cholesky(matrix[start:start + width, start:start + width])
        below = matrix[start + width:, start:start + width]
        solved = jax.scipy.linalg.solve_triangular(lower, below.T, lower=True).T
        whole = jnp.concatenate([jnp.zeros((start, width), matrix.dtype), lower, solved], axis=0)
        matrix = matrix - jnp.dot(whole, whole.T, precision=lax.Precision.HIGHEST)
        panels.append(whole)
    factor = jnp.concatenate(panels, axis=1)
    lead = 2 * width
    solution = jax.scipy.linalg.solve_triangular(factor[:lead], wanted[:lead], lower=True)
    rest = wanted[lead:] - jnp.dot(factor[lead:], solution, precision=lax.Precision.HIGHEST)
    updated = jnp.concatenate([solution, rest], axis=0).reshape(targets.shape)
    index = jnp.arange(order, dtype=jnp.int32)
    keep = (index[:, None] >= lead) & (index[None, :] >= lead)
    trailing = jnp.where(keep, matrix, jnp.zeros_like(matrix)).reshape(kernel.shape)
    return (factor.reshape(kernel.shape[0], kernel.shape[1], 2 * width), trailing, updated)
```

```python
import functools

import jax
import jax.numpy as jnp
from jax import lax
from jax.experimental import pallas as pl
from jax.experimental.pallas import tpu as pltpu
from jax.sharding import PartitionSpec as P

highest = lax.Precision.HIGHEST
TB = 128
LEAD = 512
TILES = LEAD // TB
PAIRS = [(i, j) for i in range(TILES) for j in range(i + 1)]
SLOT = 4 * len(PAIRS) + 16
VMEM = pl.BlockSpec(memory_space=pltpu.VMEM)
SMEM = pl.BlockSpec(memory_space=pltpu.SMEM)


def dot(a, b):
    return jnp.dot(a, b, precision=highest, preferred_element_type=jnp.float32)


def dot_nt(a, b):
    return lax.dot_general(
        a, b, (((1,), (1,)), ((), ())), precision=highest, preferred_element_type=jnp.float32
    )


def recip(p):
    r = pltpu.reciprocal(p, approx=True)
    return r * (2.0 - p * r)


def factor_tile(m_ref):
    n, w = TB, 8
    for g in range(n // w):
        base = w * g
        rows = [jnp.broadcast_to(m_ref[base + k : base + k + 1, 0:n], (8, n)) for k in range(w)]
        erow = [jnp.broadcast_to(m_ref[base + k : base + k + 1, n:], (8, n)) for k in range(w)]
        a, l, r = {}, {}, {}
        for k in range(w):
            for i in range(k + 1):
                a[k, i] = jnp.broadcast_to(rows[k][:, base + i : base + i + 1], (8, n))
        for i in range(w):
            r[i] = recip(a[i, i])
            for k in range(i + 1, w):
                l[k, i] = a[k, i] * r[i]
            for k in range(i + 1, w):
                for j in range(i + 1, k + 1):
                    a[k, j] = a[k, j] - l[k, i] * a[j, i]
                rows[k] = rows[k] - l[k, i] * rows[i]
                erow[k] = erow[k] - l[k, i] * erow[i]
        for k in range(w):
            m_ref[base + k : base + k + 1, n:] = (erow[k] * lax.rsqrt(a[k, k]))[0:1]
        if g == n // w - 1:
            break
        q = [rows[k] * r[k] for k in range(w)]
        qe = [erow[k] * r[k] for k in range(w)]
        for k in range(w - 1, -1, -1):
            for m in range(k + 1, w):
                q[k] = q[k] - l[m, k] * q[m]
                qe[k] = qe[k] - l[m, k] * qe[m]
        for rb in range(g + 1, n // w):
            d = m_ref[8 * rb : 8 * rb + 8, 0:n]
            e = m_ref[8 * rb : 8 * rb + 8, n:]
            cols = [jnp.broadcast_to(d[:, base + k : base + k + 1], (8, n)) for k in range(w)]
            for k in range(w):
                d = d - cols[k] * q[k]
                e = e - cols[k] * qe[k]
            m_ref[8 * rb : 8 * rb + 8, 0:n] = d
            m_ref[8 * rb : 8 * rb + 8, n:] = e


def chol_kernel(slots_ref, x_ref, s_ref, m_ref):
    n = TB
    for p, (i, j) in enumerate(PAIRS):
        for t in range(32):
            s_ref[n * i + 4 * t : n * i + 4 * t + 4, n * j : n * j + n] = slots_ref[
                SLOT * t + 4 * p : SLOT * t + 4 * p + 4, :
            ]
    eye = (
        lax.broadcasted_iota(jnp.int32, (n, n), 0) == lax.broadcasted_iota(jnp.int32, (n, n), 1)
    ).astype(jnp.float32)
    for k in range(TILES):
        sl = slice(n * k, n * k + n)
        m_ref[:, 0:n] = s_ref[sl, sl]
        m_ref[:, n:] = eye
        factor_tile(m_ref)
        inv = m_ref[:, n:]
        if k > 0:
            x_ref[sl, 0 : n * k] = -dot(inv, dot(s_ref[sl, 0 : n * k], x_ref[0 : n * k, 0 : n * k]))
        x_ref[sl, sl] = inv
        if k < TILES - 1:
            x_ref[sl, n * (k + 1) :] = jnp.zeros((n, LEAD - n * (k + 1)), jnp.float32)
            low = dot_nt(s_ref[n * (k + 1) :, sl], inv)
            s_ref[n * (k + 1) :, sl] = low
            for j in range(k + 1, TILES):
                o = n * (j - k - 1)
                s_ref[n * j :, n * j : n * j + n] = s_ref[n * j :, n * j : n * j + n] - dot_nt(
                    low[o:], low[o : o + n]
                )


def final_kernel(
    ids_ref, x_ref, slots_ref, kernel_ref,
    p0, p1, p2, p3, v0, v1, v2, v3,
    factor_ref, out_ref, z_ref,
    p_ref, v_ref, f_ref, y_ref, w_ref,
):
    n = TB
    my_row, my_col = ids_ref[0], ids_ref[1]
    x, core = lax.rem(my_row, 4), lax.rem(my_col, 2)
    group = lax.rem(my_col, 4)
    for k, src in enumerate((p0, p1, p2, p3)):
        p_ref[:, pl.ds(pl.multiple_of((group ^ k) * n, n), n)] = src[...]
    for k, src in enumerate((v0, v1, v2, v3)):
        at = pl.ds(pl.multiple_of((x ^ k) * n, n), n)
        for b in range(8):
            v_ref[at, n * b : n * b + n] = src[pl.ds(b, n, stride=8), :]
    for i in range(TILES):
        for c in range(16):
            y_ref[n * i + 8 * c : n * i + 8 * c + 8, :] = slots_ref[
                pl.ds(8 * i * SLOT + 4 * len(PAIRS) + c, 8, stride=SLOT), :
            ]
    row = lax.broadcasted_iota(jnp.int32, (LEAD, n), 0)
    col = lax.broadcasted_iota(jnp.int32, (LEAD, n), 1)
    whole_row = (row // n * 32 + my_row) * n + lax.rem(row, n)
    for i in range(TILES):
        upto = n * (i + 1)
        sl = slice(n * i, upto)
        inv = x_ref[sl, 0:upto]
        f = dot_nt(p_ref[:, 0:upto], inv)
        factor_ref[:, sl] = jnp.where(col + n * i <= whole_row, f, 0.0)
        w_ref[sl, :] = dot(inv, y_ref[0:upto, :])
        f_ref[sl, :] = dot(inv, v_ref[0:upto, :])
    z_ref[...] = dot(factor_ref[pl.ds(pl.multiple_of(core * 256, 256), 256), :], w_ref[...])

    @pl.when((my_row < TILES) & (core == 0))
    def _():
        z_ref[0:n, :] = w_ref[pl.ds(pl.multiple_of(my_row * n, n), n), :]

    @pl.loop(0, 4)
    def _(h):
        update = dot(factor_ref[...], f_ref[:, pl.ds(pl.multiple_of(h * 256, 256), 256)])
        for half in range(2):
            b = 2 * h + half
            at = pl.ds(b, LEAD, stride=8)
            left = kernel_ref[at, :] - update[:, n * half : n * half + n]
            drop = ((row < n) & (my_row < TILES)) | ((b == 0) & (my_col < TILES))
            out_ref[at, :] = jnp.where(drop, 0.0, left)


def per_device(kernel, targets):
    my_row = lax.axis_index("row")
    my_col = lax.axis_index("col")
    f32 = jnp.float32

    own = kernel[:, :, 0, :].reshape(LEAD, TB)
    got = [lax.ppermute(own, "col", [(c, c + d) for c in range(4)]) for d in (4, 8, 12)]
    own = jnp.where(my_col < 4, own, got[0] + got[1] + got[2])
    panel = [own] + [lax.ppermute(own, "col", [(c, c ^ k) for c in range(16)]) for k in (1, 2, 3)]

    lead = kernel[0].reshape(8 * TB, TB)
    have = [0]
    for d in (16, 8, 4):
        got = lax.ppermute(lead, "row", [(z + x, z + x + d) for z in have for x in range(4)])
        new = functools.reduce(jnp.logical_or, [my_row // 4 == (z + d) // 4 for z in have])
        lead = jnp.where(new, got, lead)
        have = have + [z + d for z in have]
    leads = [lead] + [lax.ppermute(lead, "row", [(r, r ^ k) for r in range(32)]) for k in (1, 2, 3)]

    tile = kernel[0, :, 0, :].reshape(32, 4, TB)
    wide = targets[0, 0].reshape(8, 8, TB)
    wide = jnp.broadcast_to(wide[None], (4, 8, 8, TB)).reshape(32, 8, TB)
    got = lax.all_to_all(jnp.concatenate([tile, wide], axis=1), "row", 0, 0)
    part = got[0:4, 0:4].reshape(1, 16, TB)
    wide = lax.dynamic_index_in_dim(got, my_row // 8, 0, keepdims=False)[4:12]
    send = jnp.concatenate(
        [jnp.broadcast_to(part, (16, 16, TB)), jnp.repeat(wide, 2, axis=0)[:, None]], axis=1
    )
    got = lax.all_to_all(send, "col", 0, 0)
    part = got[0:4, 0:16].reshape(4, 4, 4, TB)
    slot = jnp.concatenate([part[j, i] for i, j in PAIRS] + [got[:, 16]], axis=0)
    slots = lax.all_to_all(jnp.broadcast_to(slot[None], (32, SLOT, TB)), "row", 0, 0)
    slots = slots.reshape(32 * SLOT, TB)

    inverse = pl.pallas_call(
        chol_kernel,
        out_shape=jax.ShapeDtypeStruct((LEAD, LEAD), f32),
        in_specs=[VMEM],
        out_specs=VMEM,
        scratch_shapes=[pltpu.VMEM((LEAD, LEAD), f32), pltpu.VMEM((TB, 2 * TB), f32)],
        compiler_params=pltpu.CompilerParams(vmem_limit_bytes=16 << 20),
        cost_estimate=pl.CostEstimate(flops=2 * 10**10, bytes_accessed=3 << 20, transcendentals=0),
    )(slots)

    ids = jnp.stack([my_row, my_col]).astype(jnp.int32)
    factor, trailing, z = pl.pallas_call(
        final_kernel,
        out_shape=[
            jax.ShapeDtypeStruct((LEAD, LEAD), f32),
            jax.ShapeDtypeStruct((8 * LEAD, TB), f32),
            jax.ShapeDtypeStruct((2 * TB, TB), f32),
        ],
        in_specs=[SMEM] + [VMEM] * 11,
        out_specs=[VMEM] * 3,
        scratch_shapes=[
            pltpu.VMEM((LEAD, LEAD), f32),
            pltpu.VMEM((LEAD, 8 * TB), f32),
            pltpu.VMEM((LEAD, 8 * TB), f32),
            pltpu.VMEM((LEAD, TB), f32),
            pltpu.VMEM((LEAD, TB), f32),
        ],
        compiler_params=pltpu.CompilerParams(vmem_limit_bytes=40 << 20),
        cost_estimate=pl.CostEstimate(flops=10**10, bytes_accessed=10 << 20, transcendentals=0),
    )(ids, inverse, slots, kernel.reshape(8 * LEAD, TB), *panel, *leads)

    send = z.reshape(2, 16, 8, TB).transpose(1, 0, 2, 3)
    got = lax.all_to_all(send, "col", 0, 0).reshape(8, 2, 2, 8, TB)
    got = got.transpose(1, 2, 3, 0, 4).reshape(4, 8, 8 * TB)
    top = (jnp.arange(4, dtype=jnp.int32) == 0)[:, None, None] & (my_row < TILES)
    targets_out = jnp.where(top, got, targets[:, 0] - got)[:, None]
    return (
        factor.reshape(4, TB, LEAD),
        trailing.reshape(kernel.shape),
        targets_out,
    )


def solution(mesh):
    return jax.shard_map(
        per_device,
        mesh=mesh,
        in_specs=(P(None, "row", None, "col"), P(None, "row", "col", None)),
        out_specs=(P(None, "row", None), P(None, "row", None, "col"), P(None, "row", "col", None)),
        check_vma=False,
    )
```

```python
import functools

import jax
import jax.numpy as jnp
from jax import lax
from jax.experimental import pallas as pl
from jax.experimental.pallas import tpu as pltpu
from jax.sharding import PartitionSpec as P

highest = lax.Precision.HIGHEST
TB = 128
LEAD = 512
TILES = LEAD // TB
ORDER = (0, 1, 3, 2)
BIG = 56 << 20
VMEM = pl.BlockSpec(memory_space=pltpu.VMEM)
HBM = pl.BlockSpec(memory_space=pltpu.HBM)
SMEM = pl.BlockSpec(memory_space=pltpu.SMEM)


def dot(a, b):
    return jnp.dot(a, b, precision=highest, preferred_element_type=jnp.float32)


def dot_nt(a, b):
    return lax.dot_general(
        a, b, (((1,), (1,)), ((), ())), precision=highest, preferred_element_type=jnp.float32
    )


def recip(p):
    r = pltpu.reciprocal(p, approx=True)
    return r * (2.0 - p * r)


def factor_tile(m_ref):
    n, w = TB, 8
    for g in range(n // w):
        base = w * g
        rows = [jnp.broadcast_to(m_ref[base + k : base + k + 1, 0:n], (8, n)) for k in range(w)]
        erow = [jnp.broadcast_to(m_ref[base + k : base + k + 1, n:], (8, n)) for k in range(w)]
        a, l, r = {}, {}, {}
        for k in range(w):
            for i in range(k + 1):
                a[k, i] = jnp.broadcast_to(rows[k][:, base + i : base + i + 1], (8, n))
        for i in range(w):
            r[i] = recip(a[i, i])
            for k in range(i + 1, w):
                l[k, i] = a[k, i] * r[i]
            for k in range(i + 1, w):
                for j in range(i + 1, k + 1):
                    a[k, j] = a[k, j] - l[k, i] * a[j, i]
                rows[k] = rows[k] - l[k, i] * rows[i]
                erow[k] = erow[k] - l[k, i] * erow[i]
        for k in range(w):
            m_ref[base + k : base + k + 1, n:] = (erow[k] * lax.rsqrt(a[k, k]))[0:1]
        if g == n // w - 1:
            break
        q = [rows[k] * r[k] for k in range(w)]
        qe = [erow[k] * r[k] for k in range(w)]
        for k in range(w - 1, -1, -1):
            for m in range(k + 1, w):
                q[k] = q[k] - l[m, k] * q[m]
                qe[k] = qe[k] - l[m, k] * qe[m]
        for rb in range(g + 1, n // w):
            d = m_ref[8 * rb : 8 * rb + 8, 0:n]
            e = m_ref[8 * rb : 8 * rb + 8, n:]
            cols = [jnp.broadcast_to(d[:, base + k : base + k + 1], (8, n)) for k in range(w)]
            for k in range(w):
                d = d - cols[k] * q[k]
                e = e - cols[k] * qe[k]
            m_ref[8 * rb : 8 * rb + 8, 0:n] = d
            m_ref[8 * rb : 8 * rb + 8, n:] = e


def chol_kernel(ids_ref, t0, t1, t2, t3, x_hbm, x_ref, s_ref, m_ref, sem):
    n = TB
    x, group = lax.rem(ids_ref[0], 4), lax.rem(ids_ref[1], 4)
    for m, src in enumerate((t0, t1, t2, t3)):
        for at, k in enumerate(ORDER):
            rows = pl.ds(pl.multiple_of((x ^ k) * n, n), n)
            cols = pl.ds(pl.multiple_of((group ^ m) * n, n), n)
            s_ref[rows, cols] = src[n * at : n * at + n, :]
    eye = (
        lax.broadcasted_iota(jnp.int32, (n, n), 0) == lax.broadcasted_iota(jnp.int32, (n, n), 1)
    ).astype(jnp.float32)
    for k in range(TILES):
        sl = slice(n * k, n * k + n)
        m_ref[:, 0:n] = s_ref[sl, sl]
        m_ref[:, n:] = eye
        factor_tile(m_ref)
        inv = m_ref[:, n:]
        if k > 0:
            x_ref[sl, 0 : n * k] = -dot(inv, dot(s_ref[sl, 0 : n * k], x_ref[0 : n * k, 0 : n * k]))
        x_ref[sl, sl] = inv
        if k < TILES - 1:
            x_ref[sl, n * (k + 1) :] = jnp.zeros((n, LEAD - n * (k + 1)), jnp.float32)
            low = dot_nt(s_ref[n * (k + 1) :, sl], inv)
            s_ref[n * (k + 1) :, sl] = low
            for j in range(k + 1, TILES):
                o = n * (j - k - 1)
                s_ref[n * j :, n * j : n * j + n] = s_ref[n * j :, n * j : n * j + n] - dot_nt(
                    low[o:], low[o : o + n]
                )
    put_x = pltpu.make_async_copy(x_ref, x_hbm, sem.at[0])
    put_x.start()
    put_x.wait()


def panel_kernel(
    ids_ref, x_hbm, y_hbm, p0, p2, p13, factor_hbm, z_ref, x_ref, raw_ref, factor_ref, p_ref, y_ref, w_ref, sem
):
    n = TB
    my_row, core = ids_ref[0], lax.rem(ids_ref[1], 2)
    x, group = lax.rem(my_row, 4), lax.rem(ids_ref[1], 4)
    gets = [pltpu.make_async_copy(x_hbm, x_ref, sem.at[0]), pltpu.make_async_copy(y_hbm, raw_ref, sem.at[1])]
    for k, src in ((0, p0), (1, p13.at[0:LEAD]), (2, p2), (3, p13.at[LEAD:])):
        cols = pl.ds(pl.multiple_of((group ^ k) * n, n), n)
        gets.append(pltpu.make_async_copy(src, p_ref.at[:, cols], sem.at[2 + k]))
    for get in gets:
        get.start()
    for get in gets:
        get.wait()
    for at, k in enumerate(ORDER):
        for c in range(16):
            y_ref[pl.ds(pl.multiple_of((x ^ k) * n + 8 * c, 8), 8), :] = raw_ref[c, 8 * at : 8 * at + 8, :]
    row = lax.broadcasted_iota(jnp.int32, (LEAD, n), 0)
    col = lax.broadcasted_iota(jnp.int32, (LEAD, n), 1)
    whole_row = (row // n * 32 + my_row) * n + lax.rem(row, n)
    for i in range(TILES):
        upto = n * (i + 1)
        sl = slice(n * i, upto)
        inv = x_ref[sl, 0:upto]
        f = dot_nt(p_ref[:, 0:upto], inv)
        factor_ref[:, sl] = jnp.where(col + n * i <= whole_row, f, 0.0)
        w_ref[sl, :] = dot(inv, y_ref[0:upto, :])
    put = pltpu.make_async_copy(factor_ref, factor_hbm, sem.at[6])
    put.start()
    z = dot(factor_ref[pl.ds(pl.multiple_of(core * 256, 256), 256), :], w_ref[...])
    for a in range(2):
        for c in range(16):
            z_ref[16 * c + 8 * a : 16 * c + 8 * a + 8, :] = z[n * a + 8 * c : n * a + 8 * c + 8]

    @pl.when((my_row < TILES) & (core == 0))
    def _():
        for c in range(16):
            at = pl.multiple_of(my_row * n + 8 * c, 8)
            z_ref[16 * c : 16 * c + 8, :] = w_ref[pl.ds(at, 8), :]
    put.wait()


def trailing_kernel(
    ids_ref, x_hbm, factor_hbm, kernel_hbm, v0_hbm, v1_hbm, v2_hbm, v3_hbm, out_hbm,
    x_ref, factor_ref, kernel_ref, raw_ref, v_ref, f_ref, out_ref, sem,
):
    n = TB
    my_row, my_col = ids_ref[0], ids_ref[1]
    x = lax.rem(my_row, 4)
    gets = [
        pltpu.make_async_copy(src, raw_ref.at[k], sem.at[k])
        for k, src in enumerate((v0_hbm, v1_hbm, v2_hbm, v3_hbm))
    ]
    get_x = pltpu.make_async_copy(x_hbm, x_ref, sem.at[4])
    get_factor = pltpu.make_async_copy(factor_hbm, factor_ref, sem.at[5])
    tiles = [pl.ds(8 * n * a, 8 * n) for a in range(4)]
    get_tiles = [
        pltpu.make_async_copy(kernel_hbm.at[at], kernel_ref.at[at], sem.at[6 + a])
        for a, at in enumerate(tiles)
    ]
    puts = [
        pltpu.make_async_copy(out_ref.at[at], out_hbm.at[at], sem.at[10 + a])
        for a, at in enumerate(tiles)
    ]
    for copy in [*gets, get_x, get_factor, *get_tiles]:
        copy.start()
    for k in range(4):
        gets[k].wait()
        at = pl.ds(pl.multiple_of((x ^ k) * n, n), n)
        for b in range(8):
            v_ref[at, n * b : n * b + n] = raw_ref[k, pl.ds(b, n, stride=8), :]
    get_x.wait()
    for i in range(TILES):
        upto = n * (i + 1)
        f_ref[n * i : upto, :] = dot(x_ref[n * i : upto, 0:upto], v_ref[0:upto, :])
    get_factor.wait()
    for a in range(4):
        get_tiles[a].wait()
        for h in range(4):
            update = dot(factor_ref[n * a : n * a + n, :], f_ref[:, 256 * h : 256 * h + 256])
            for half in range(2):
                b = 2 * h + half
                at = pl.ds(8 * n * a + b, n, stride=8)
                left = kernel_ref[at, :] - update[:, n * half : n * half + n]
                if a == 0:
                    left = jnp.where(my_row < TILES, 0.0, left)
                if b == 0:
                    left = jnp.where(my_col < TILES, 0.0, left)
                out_ref[at, :] = left
        puts[a].start()
    for put in puts:
        put.wait()


def permute_z(block, hops):
    return lax.ppermute(block, "row", [(4 * a + x, 4 * b + x) for a, b in hops for x in range(4)])


def permute_xor(block, axis, k):
    return lax.ppermute(block, axis, [(i, i ^ k) for i in range(lax.axis_size(axis))])


def tree(block, depth, first):
    up, down = ([(0, 3)], [(0, 5)]) if first else ([(0, 1), (3, 4), (5, 6)], [(0, 7), (3, 2)])

    def pick(got):
        picked = block
        for hops, new in zip((up, down), got):
            hit = jnp.any(jnp.stack([depth == b for _, b in hops]))
            picked = jnp.where(hit, new, picked)
        return picked

    return [permute_z(block, up), permute_z(block, down)], pick


def per_device(kernel, targets):
    my_row = lax.axis_index("row")
    my_col = lax.axis_index("col")
    depth = my_row // 4
    f32 = jnp.float32
    ids = jnp.stack([my_row, my_col]).astype(jnp.int32)
    force = lax.optimization_barrier

    tile = kernel[0, :, 0, :]
    got = [lax.ppermute(tile, "col", [(c, c + d) for c in range(4)]) for d in (4, 8, 12)]
    tile = jnp.where(my_col < 4, tile, got[0] + got[1] + got[2])
    block = jnp.concatenate([tile, targets[0, 0].reshape(64, TB)], axis=0)
    got, pick = tree(block, depth, True)
    own = kernel[:, :, 0, :].reshape(LEAD, TB)
    block = pick(got)
    got, pick = tree(block, depth, False)
    own_got = lax.ppermute(own, "col", [(c, c + 8) for c in range(4)])
    got, own_got = force((got, own_got))
    block = pick(got)
    own = jnp.where((my_col >= 8) & (my_col < 12), own_got, own)

    block_1 = permute_xor(block, "row", 1)
    block_32 = permute_xor(jnp.concatenate([block, block_1], axis=0), "row", 3)
    lead = kernel[0].reshape(8 * TB, TB)
    got, pick = tree(lead, depth, True)
    own_got = lax.ppermute(own, "col", [(c, c + 4) for c in (0, 1, 2, 3, 8, 9, 10, 11)])
    block_32, got, own_got = force((block_32, got, own_got))
    lead = pick(got)
    own = jnp.where(my_col % 8 >= 4, own_got, own)
    blocks = [block, block_1, block_32[:192], block_32[192:]]

    t0 = jnp.concatenate([b[:TB] for b in blocks], axis=0)
    t2, t1 = permute_xor(t0, "col", 2), permute_xor(t0, "col", 1)
    got, pick = tree(lead, depth, False)
    own_2 = permute_xor(own, "col", 2)
    wide = jnp.stack([b[TB:].reshape(8, 8, TB) for b in blocks]).transpose(2, 0, 1, 3)
    wide = lax.all_to_all(jnp.repeat(wide.reshape(8, 32, TB), 2, axis=0), "col", 0, 0)
    t3 = permute_xor(t2, "col", 1)
    t1, t3, got, own_2, wide = force((t1, t3, got, own_2, wide))
    lead = pick(got)
    own_13 = permute_xor(jnp.concatenate([own, own_2], axis=0), "col", 1)
    leads = [lead] + [permute_xor(lead, "row", k) for k in (1, 2, 3)]

    inverse = pl.pallas_call(
        chol_kernel,
        out_shape=jax.ShapeDtypeStruct((LEAD, LEAD), f32),
        in_specs=[SMEM] + [VMEM] * 4,
        out_specs=HBM,
        scratch_shapes=[
            pltpu.VMEM((LEAD, LEAD), f32),
            pltpu.VMEM((LEAD, LEAD), f32),
            pltpu.VMEM((TB, 2 * TB), f32),
            pltpu.SemaphoreType.DMA((1,)),
        ],
        compiler_params=pltpu.CompilerParams(vmem_limit_bytes=BIG),
        cost_estimate=pl.CostEstimate(flops=2 * 10**10, bytes_accessed=3 << 20, transcendentals=0),
    )(ids, t0, t1, t2, t3)

    factor, z = pl.pallas_call(
        panel_kernel,
        out_shape=[
            jax.ShapeDtypeStruct((LEAD, LEAD), f32),
            jax.ShapeDtypeStruct((2 * TB, TB), f32),
        ],
        in_specs=[SMEM] + [HBM] * 5,
        out_specs=[HBM, VMEM],
        scratch_shapes=[
            pltpu.VMEM((LEAD, LEAD), f32),
            pltpu.VMEM((16, 32, TB), f32),
            pltpu.VMEM((LEAD, LEAD), f32),
            pltpu.VMEM((LEAD, LEAD), f32),
            pltpu.VMEM((LEAD, TB), f32),
            pltpu.VMEM((LEAD, TB), f32),
            pltpu.SemaphoreType.DMA((7,)),
        ],
        compiler_params=pltpu.CompilerParams(vmem_limit_bytes=BIG),
        cost_estimate=pl.CostEstimate(flops=2 * 10**9, bytes_accessed=4 << 20, transcendentals=0),
    )(ids, inverse, wide, own, own_2, own_13)

    trailing = pl.pallas_call(
        trailing_kernel,
        out_shape=jax.ShapeDtypeStruct((8 * LEAD, TB), f32),
        in_specs=[SMEM] + [HBM] * 7,
        out_specs=HBM,
        scratch_shapes=[
            pltpu.VMEM((LEAD, LEAD), f32),
            pltpu.VMEM((LEAD, LEAD), f32),
            pltpu.VMEM((8 * LEAD, TB), f32),
            pltpu.VMEM((4, 8 * TB, TB), f32),
            pltpu.VMEM((LEAD, 8 * TB), f32),
            pltpu.VMEM((LEAD, 8 * TB), f32),
            pltpu.VMEM((8 * LEAD, TB), f32),
            pltpu.SemaphoreType.DMA((14,)),
        ],
        compiler_params=pltpu.CompilerParams(vmem_limit_bytes=BIG),
        cost_estimate=pl.CostEstimate(flops=10**10, bytes_accessed=10 << 20, transcendentals=0),
    )(ids, inverse, factor, kernel.reshape(8 * LEAD, TB), *leads)

    got = lax.all_to_all(z.reshape(16, 2, 8, TB), "col", 0, 0).reshape(8, 2, 2, 8, TB)
    got = got.transpose(1, 2, 3, 0, 4).reshape(4, 8, 8 * TB)
    top = (jnp.arange(4, dtype=jnp.int32) == 0)[:, None, None] & (my_row < TILES)
    targets_out = jnp.where(top, got, targets[:, 0] - got)[:, None]
    return (
        factor.reshape(4, TB, LEAD),
        trailing.reshape(kernel.shape),
        targets_out,
    )


def solution(mesh):
    return jax.shard_map(
        per_device,
        mesh=mesh,
        in_specs=(P(None, "row", None, "col"), P(None, "row", "col", None)),
        out_specs=(P(None, "row", None), P(None, "row", None, "col"), P(None, "row", "col", None)),
        check_vma=False,
    )
```

```python
import functools

import jax
import jax.numpy as jnp
from jax import lax
from jax.experimental import pallas as pl
from jax.experimental.pallas import tpu as pltpu
from jax.sharding import PartitionSpec as P

highest = lax.Precision.HIGHEST
TB = 128
LEAD = 512
TILES = LEAD // TB
ORDER = (0, 1, 3, 2)
BIG = 56 << 20
VMEM = pl.BlockSpec(memory_space=pltpu.VMEM)
HBM = pl.BlockSpec(memory_space=pltpu.HBM)
SMEM = pl.BlockSpec(memory_space=pltpu.SMEM)


def dot(a, b):
    return jnp.dot(a, b, precision=highest, preferred_element_type=jnp.float32)


def dot_nt(a, b):
    return lax.dot_general(
        a, b, (((1,), (1,)), ((), ())), precision=highest, preferred_element_type=jnp.float32
    )


def recip(p):
    r = pltpu.reciprocal(p, approx=True)
    return r * (2.0 - p * r)


def factor_tile(m_ref):
    n, w = TB, 8
    for g in range(n // w):
        base = w * g
        rows = [jnp.broadcast_to(m_ref[base + k : base + k + 1, 0:n], (8, n)) for k in range(w)]
        erow = [jnp.broadcast_to(m_ref[base + k : base + k + 1, n:], (8, n)) for k in range(w)]
        a, l, r = {}, {}, {}
        for k in range(w):
            for i in range(k + 1):
                a[k, i] = jnp.broadcast_to(rows[k][:, base + i : base + i + 1], (8, n))
        for i in range(w):
            r[i] = recip(a[i, i])
            for k in range(i + 1, w):
                l[k, i] = a[k, i] * r[i]
            for k in range(i + 1, w):
                for j in range(i + 1, k + 1):
                    a[k, j] = a[k, j] - l[k, i] * a[j, i]
                rows[k] = rows[k] - l[k, i] * rows[i]
                erow[k] = erow[k] - l[k, i] * erow[i]
        for k in range(w):
            m_ref[base + k : base + k + 1, n:] = (erow[k] * lax.rsqrt(a[k, k]))[0:1]
        if g == n // w - 1:
            break
        q = [rows[k] * r[k] for k in range(w)]
        qe = [erow[k] * r[k] for k in range(w)]
        for k in range(w - 1, -1, -1):
            for m in range(k + 1, w):
                q[k] = q[k] - l[m, k] * q[m]
                qe[k] = qe[k] - l[m, k] * qe[m]
        for rb in range(g + 1, n // w):
            d = m_ref[8 * rb : 8 * rb + 8, 0:n]
            e = m_ref[8 * rb : 8 * rb + 8, n:]
            cols = [jnp.broadcast_to(d[:, base + k : base + k + 1], (8, n)) for k in range(w)]
            for k in range(w):
                d = d - cols[k] * q[k]
                e = e - cols[k] * qe[k]
            m_ref[8 * rb : 8 * rb + 8, 0:n] = d
            m_ref[8 * rb : 8 * rb + 8, n:] = e


def chol_kernel(ids_ref, t0, t1, t2, t3, x_hbm, x_ref, s_ref, m_ref, sem):
    n = TB
    x, group = lax.rem(ids_ref[0], 4), lax.rem(ids_ref[1], 4)
    for m, src in enumerate((t0, t1, t2, t3)):
        for at, k in enumerate(ORDER):
            rows = pl.ds(pl.multiple_of((x ^ k) * n, n), n)
            cols = pl.ds(pl.multiple_of((group ^ m) * n, n), n)
            s_ref[rows, cols] = src[n * at : n * at + n, :]
    eye = (
        lax.broadcasted_iota(jnp.int32, (n, n), 0) == lax.broadcasted_iota(jnp.int32, (n, n), 1)
    ).astype(jnp.float32)
    for k in range(TILES):
        sl = slice(n * k, n * k + n)
        m_ref[:, 0:n] = s_ref[sl, sl]
        m_ref[:, n:] = eye
        factor_tile(m_ref)
        inv = m_ref[:, n:]
        if k > 0:
            x_ref[sl, 0 : n * k] = -dot(inv, dot(s_ref[sl, 0 : n * k], x_ref[0 : n * k, 0 : n * k]))
        x_ref[sl, sl] = inv
        if k < TILES - 1:
            x_ref[sl, n * (k + 1) :] = jnp.zeros((n, LEAD - n * (k + 1)), jnp.float32)
            low = dot_nt(s_ref[n * (k + 1) :, sl], inv)
            s_ref[n * (k + 1) :, sl] = low
            for j in range(k + 1, TILES):
                o = n * (j - k - 1)
                s_ref[n * j :, n * j : n * j + n] = s_ref[n * j :, n * j : n * j + n] - dot_nt(
                    low[o:], low[o : o + n]
                )
    put_x = pltpu.make_async_copy(x_ref, x_hbm, sem.at[0])
    put_x.start()
    put_x.wait()


def panel_kernel(
    ids_ref, x_hbm, y_hbm, p0, p1, p2, p3, factor_hbm, z_ref, x_ref, raw_ref, factor_ref, p_ref, y_ref, w_ref, sem
):
    n = TB
    my_row, core = ids_ref[0], lax.rem(ids_ref[1], 2)
    x, group = lax.rem(my_row, 4), lax.rem(ids_ref[1], 4)
    gets = [pltpu.make_async_copy(x_hbm, x_ref, sem.at[0]), pltpu.make_async_copy(y_hbm, raw_ref, sem.at[1])]
    for k, src in enumerate((p0, p1, p2, p3)):
        cols = pl.ds(pl.multiple_of((group ^ k) * n, n), n)
        gets.append(pltpu.make_async_copy(src, p_ref.at[:, cols], sem.at[2 + k]))
    for get in gets:
        get.start()
    for get in gets:
        get.wait()
    for at, k in enumerate(ORDER):
        for c in range(16):
            y_ref[pl.ds(pl.multiple_of((x ^ k) * n + 8 * c, 8), 8), :] = raw_ref[c, 8 * at : 8 * at + 8, :]
    for i in range(0, LEAD, 2 * n):
        sl, upto = slice(i, i + 2 * n), i + 2 * n
        inv = x_ref[sl, 0:upto]
        w_ref[sl, :] = dot(inv, y_ref[0:upto, :])
        factor_ref[:, sl] = dot_nt(p_ref[:, 0:upto], inv)

    @pl.when(my_row < TILES)
    def _():
        row = lax.broadcasted_iota(jnp.int32, (n, LEAD), 0) + my_row * n
        lower = lax.broadcasted_iota(jnp.int32, (n, LEAD), 1) <= row
        factor_ref[0:n, :] = jnp.where(lower, factor_ref[0:n, :], 0.0)

    put = pltpu.make_async_copy(factor_ref, factor_hbm, sem.at[6])
    put.start()
    z = dot(factor_ref[pl.ds(pl.multiple_of(core * 256, 256), 256), :], w_ref[...])
    for a in range(2):
        for c in range(16):
            z_ref[16 * c + 8 * a : 16 * c + 8 * a + 8, :] = z[n * a + 8 * c : n * a + 8 * c + 8]

    @pl.when((my_row < TILES) & (core == 0))
    def _():
        for c in range(16):
            at = pl.multiple_of(my_row * n + 8 * c, 8)
            z_ref[16 * c : 16 * c + 8, :] = w_ref[pl.ds(at, 8), :]
    put.wait()


def trailing_kernel(
    ids_ref, x_hbm, factor_hbm, kernel_hbm, v_hbm, out_hbm,
    x_ref, factor_ref, kernel_ref, raw_ref, v_ref, f_ref, out_ref, sem,
):
    n = TB
    my_row, my_col = ids_ref[0], ids_ref[1]
    gets = [pltpu.make_async_copy(v_hbm.at[k], raw_ref.at[k], sem.at[k]) for k in range(4)]
    get_x = pltpu.make_async_copy(x_hbm, x_ref, sem.at[4])
    get_factor = pltpu.make_async_copy(factor_hbm, factor_ref, sem.at[5])
    tiles = [pl.ds(8 * n * a, 8 * n) for a in range(4)]
    get_tiles = [
        pltpu.make_async_copy(kernel_hbm.at[at], kernel_ref.at[at], sem.at[6 + a])
        for a, at in enumerate(tiles)
    ]
    puts = [
        pltpu.make_async_copy(out_ref.at[at], out_hbm.at[at], sem.at[10 + a])
        for a, at in enumerate(tiles)
    ]
    for copy in [*gets, get_x, get_factor, *get_tiles]:
        copy.start()
    for k in range(4):
        gets[k].wait()
        for b in range(8):
            v_ref[n * k : n * k + n, n * b : n * b + n] = raw_ref[k, pl.ds(b, n, stride=8), :]
    get_x.wait()
    for i in range(0, LEAD, 2 * n):
        upto = i + 2 * n
        f_ref[i:upto, :] = dot(x_ref[i:upto, 0:upto], v_ref[0:upto, :])
    get_factor.wait()
    for pair in range(2):
        get_tiles[2 * pair].wait()
        get_tiles[2 * pair + 1].wait()
        for h in range(4):
            update = dot(
                factor_ref[2 * n * pair : 2 * n * pair + 2 * n, :], f_ref[:, 256 * h : 256 * h + 256]
            )
            for up, half in ((0, 0), (0, 1), (1, 0), (1, 1)):
                a, b = 2 * pair + up, 2 * h + half
                at = pl.ds(8 * n * a + b, n, stride=8)
                left = kernel_ref[at, :] - update[n * up : n * up + n, n * half : n * half + n]
                if a == 0:
                    left = jnp.where(my_row < TILES, 0.0, left)
                if b == 0:
                    left = jnp.where(my_col < TILES, 0.0, left)
                out_ref[at, :] = left
        puts[2 * pair].start()
        puts[2 * pair + 1].start()
    for put in puts:
        put.wait()


def permute_z(block, hops):
    return lax.ppermute(block, "row", [(4 * a + x, 4 * b + x) for a, b in hops for x in range(4)])


def permute_xor(block, axis, k):
    return lax.ppermute(block, axis, [(i, i ^ k) for i in range(lax.axis_size(axis))])


def tree(block, depth, first):
    up, down = ([(0, 3)], [(0, 5)]) if first else ([(0, 1), (3, 4), (5, 6)], [(0, 7), (3, 2)])

    def pick(got):
        picked = block
        for hops, new in zip((up, down), got):
            hit = jnp.any(jnp.stack([depth == b for _, b in hops]))
            picked = jnp.where(hit, new, picked)
        return picked

    return [permute_z(block, up), permute_z(block, down)], pick


def per_device(kernel, targets):
    my_row = lax.axis_index("row")
    my_col = lax.axis_index("col")
    depth = my_row // 4
    f32 = jnp.float32
    ids = jnp.stack([my_row, my_col]).astype(jnp.int32)
    force = lax.optimization_barrier

    tile = kernel[0, :, 0, :]
    got = [lax.ppermute(tile, "col", [(c, c + d) for c in range(4)]) for d in (4, 8, 12)]
    tile = jnp.where(my_col < 4, tile, got[0] + got[1] + got[2])
    block = jnp.concatenate([tile, targets[0, 0].reshape(64, TB)], axis=0)
    got, pick = tree(block, depth, True)
    own = kernel[:, :, 0, :].reshape(LEAD, TB)
    block = pick(got)
    got, pick = tree(block, depth, False)
    own_got = lax.ppermute(own, "col", [(c, c + 8) for c in range(4)])
    got, own_got = force((got, own_got))
    block = pick(got)
    own = jnp.where((my_col >= 8) & (my_col < 12), own_got, own)

    block_1 = permute_xor(block, "row", 1)
    block_32 = permute_xor(jnp.concatenate([block, block_1], axis=0), "row", 3)
    lead = kernel[0].reshape(8 * TB, TB)
    got, pick = tree(lead, depth, True)
    own_got = lax.ppermute(own, "col", [(c, c + 4) for c in (0, 1, 2, 3, 8, 9, 10, 11)])
    block_32, got, own_got = force((block_32, got, own_got))
    lead = pick(got)
    own = jnp.where(my_col % 8 >= 4, own_got, own)
    blocks = [block, block_1, block_32[:192], block_32[192:]]

    t0 = jnp.concatenate([b[:TB] for b in blocks], axis=0)
    t2, t1 = permute_xor(t0, "col", 2), permute_xor(t0, "col", 1)
    got, pick = tree(lead, depth, False)
    wide = jnp.stack([b[TB:].reshape(8, 8, TB) for b in blocks]).transpose(2, 0, 1, 3)
    wide = lax.all_to_all(jnp.repeat(wide.reshape(8, 32, TB), 2, axis=0), "col", 0, 0)
    t3 = permute_xor(t2, "col", 1)
    t1, t3, got, wide = force((t1, t3, got, wide))
    panel = [own] + [permute_xor(own, "col", k) for k in (1, 2, 3)]
    leads = jnp.broadcast_to(pick(got)[None], (4, 8 * TB, TB))
    groups = [[4 * z + x for x in range(4)] for z in range(lax.axis_size("row") // 4)]
    leads = lax.all_to_all(leads, "row", 0, 0, axis_index_groups=groups)

    inverse = pl.pallas_call(
        chol_kernel,
        out_shape=jax.ShapeDtypeStruct((LEAD, LEAD), f32),
        in_specs=[SMEM] + [VMEM] * 4,
        out_specs=HBM,
        scratch_shapes=[
            pltpu.VMEM((LEAD, LEAD), f32),
            pltpu.VMEM((LEAD, LEAD), f32),
            pltpu.VMEM((TB, 2 * TB), f32),
            pltpu.SemaphoreType.DMA((1,)),
        ],
        compiler_params=pltpu.CompilerParams(vmem_limit_bytes=BIG),
        cost_estimate=pl.CostEstimate(flops=2 * 10**10, bytes_accessed=3 << 20, transcendentals=0),
    )(ids, t0, t1, t2, t3)
    inverse, leads = force((inverse, leads))

    factor, z = pl.pallas_call(
        panel_kernel,
        out_shape=[
            jax.ShapeDtypeStruct((LEAD, LEAD), f32),
            jax.ShapeDtypeStruct((2 * TB, TB), f32),
        ],
        in_specs=[SMEM] + [HBM] * 6,
        out_specs=[HBM, VMEM],
        scratch_shapes=[
            pltpu.VMEM((LEAD, LEAD), f32),
            pltpu.VMEM((16, 32, TB), f32),
            pltpu.VMEM((LEAD, LEAD), f32),
            pltpu.VMEM((LEAD, LEAD), f32),
            pltpu.VMEM((LEAD, TB), f32),
            pltpu.VMEM((LEAD, TB), f32),
            pltpu.SemaphoreType.DMA((7,)),
        ],
        compiler_params=pltpu.CompilerParams(vmem_limit_bytes=BIG),
        cost_estimate=pl.CostEstimate(flops=2 * 10**9, bytes_accessed=4 << 20, transcendentals=0),
    )(ids, inverse, wide, *panel)

    trailing = pl.pallas_call(
        trailing_kernel,
        out_shape=jax.ShapeDtypeStruct((8 * LEAD, TB), f32),
        in_specs=[SMEM] + [HBM] * 4,
        out_specs=HBM,
        scratch_shapes=[
            pltpu.VMEM((LEAD, LEAD), f32),
            pltpu.VMEM((LEAD, LEAD), f32),
            pltpu.VMEM((8 * LEAD, TB), f32),
            pltpu.VMEM((4, 8 * TB, TB), f32),
            pltpu.VMEM((LEAD, 8 * TB), f32),
            pltpu.VMEM((LEAD, 8 * TB), f32),
            pltpu.VMEM((8 * LEAD, TB), f32),
            pltpu.SemaphoreType.DMA((14,)),
        ],
        compiler_params=pltpu.CompilerParams(vmem_limit_bytes=BIG),
        cost_estimate=pl.CostEstimate(flops=10**10, bytes_accessed=10 << 20, transcendentals=0),
    )(ids, inverse, factor, kernel.reshape(8 * LEAD, TB), leads)

    got = lax.all_to_all(z.reshape(16, 2, 8, TB), "col", 0, 0).reshape(8, 2, 2, 8, TB)
    got = got.transpose(1, 2, 3, 0, 4).reshape(4, 8, 8 * TB)
    top = (jnp.arange(4, dtype=jnp.int32) == 0)[:, None, None] & (my_row < TILES)
    targets_out = jnp.where(top, got, targets[:, 0] - got)[:, None]
    return (
        factor.reshape(4, TB, LEAD),
        trailing.reshape(kernel.shape),
        targets_out,
    )


def solution(mesh):
    return jax.shard_map(
        per_device,
        mesh=mesh,
        in_specs=(P(None, "row", None, "col"), P(None, "row", "col", None)),
        out_specs=(P(None, "row", None), P(None, "row", None, "col"), P(None, "row", "col", None)),
        check_vma=False,
    )
```

```python
import functools

import jax
import jax.numpy as jnp
from jax import lax
from jax.experimental import pallas as pl
from jax.experimental.pallas import tpu as pltpu
from jax.sharding import PartitionSpec as P

highest = lax.Precision.HIGHEST
TB = 128
LEAD = 512
TILES = LEAD // TB
ORDER = (0, 1, 3, 2)
BIG = 56 << 20
VMEM = pl.BlockSpec(memory_space=pltpu.VMEM)
HBM = pl.BlockSpec(memory_space=pltpu.HBM)
SMEM = pl.BlockSpec(memory_space=pltpu.SMEM)


def dot(a, b):
    return jnp.dot(a, b, precision=highest, preferred_element_type=jnp.float32)


def dot_nt(a, b):
    return lax.dot_general(
        a, b, (((1,), (1,)), ((), ())), precision=highest, preferred_element_type=jnp.float32
    )


def halves(a):
    high = a.astype(jnp.bfloat16)
    return high, (a - high.astype(jnp.float32)).astype(jnp.bfloat16)


def dot_half(a, b):
    return jnp.dot(a, b, preferred_element_type=jnp.float32)


def recip(p):
    r = pltpu.reciprocal(p, approx=True)
    return r * (2.0 - p * r)


def factor_tile(m_ref):
    n, w = TB, 8
    for g in range(n // w):
        base = w * g
        rows = [jnp.broadcast_to(m_ref[base + k : base + k + 1, 0:n], (8, n)) for k in range(w)]
        erow = [jnp.broadcast_to(m_ref[base + k : base + k + 1, n:], (8, n)) for k in range(w)]
        a, l, r = {}, {}, {}
        for k in range(w):
            for i in range(k + 1):
                a[k, i] = jnp.broadcast_to(rows[k][:, base + i : base + i + 1], (8, n))
        for i in range(w):
            r[i] = recip(a[i, i])
            for k in range(i + 1, w):
                l[k, i] = a[k, i] * r[i]
            for k in range(i + 1, w):
                for j in range(i + 1, k + 1):
                    a[k, j] = a[k, j] - l[k, i] * a[j, i]
                rows[k] = rows[k] - l[k, i] * rows[i]
                erow[k] = erow[k] - l[k, i] * erow[i]
        for k in range(w):
            m_ref[base + k : base + k + 1, n:] = (erow[k] * lax.rsqrt(a[k, k]))[0:1]
        if g == n // w - 1:
            break
        q = [rows[k] * r[k] for k in range(w)]
        qe = [erow[k] * r[k] for k in range(w)]
        for k in range(w - 1, -1, -1):
            for m in range(k + 1, w):
                q[k] = q[k] - l[m, k] * q[m]
                qe[k] = qe[k] - l[m, k] * qe[m]
        for rb in range(g + 1, n // w):
            d = m_ref[8 * rb : 8 * rb + 8, 0:n]
            e = m_ref[8 * rb : 8 * rb + 8, n:]
            cols = [jnp.broadcast_to(d[:, base + k : base + k + 1], (8, n)) for k in range(w)]
            for k in range(w):
                d = d - cols[k] * q[k]
                e = e - cols[k] * qe[k]
            m_ref[8 * rb : 8 * rb + 8, 0:n] = d
            m_ref[8 * rb : 8 * rb + 8, n:] = e


def chol_kernel(ids_ref, t0, t1, t2, t3, x_hbm, x_ref, s_ref, m_ref, sem):
    n = TB
    x, group = lax.rem(ids_ref[0], 4), lax.rem(ids_ref[1], 4)
    for m, src in enumerate((t0, t1, t2, t3)):
        for at, k in enumerate(ORDER):
            rows = pl.ds(pl.multiple_of((x ^ k) * n, n), n)
            cols = pl.ds(pl.multiple_of((group ^ m) * n, n), n)
            s_ref[rows, cols] = src[n * at : n * at + n, :]
    eye = (
        lax.broadcasted_iota(jnp.int32, (n, n), 0) == lax.broadcasted_iota(jnp.int32, (n, n), 1)
    ).astype(jnp.float32)
    for k in range(TILES):
        sl = slice(n * k, n * k + n)
        m_ref[:, 0:n] = s_ref[sl, sl]
        m_ref[:, n:] = eye
        factor_tile(m_ref)
        inv = m_ref[:, n:]
        if k > 0:
            x_ref[sl, 0 : n * k] = -dot(inv, dot(s_ref[sl, 0 : n * k], x_ref[0 : n * k, 0 : n * k]))
        x_ref[sl, sl] = inv
        if k < TILES - 1:
            x_ref[sl, n * (k + 1) :] = jnp.zeros((n, LEAD - n * (k + 1)), jnp.float32)
            low = dot_nt(s_ref[n * (k + 1) :, sl], inv)
            s_ref[n * (k + 1) :, sl] = low
            for j in range(k + 1, TILES):
                o = n * (j - k - 1)
                s_ref[n * j :, n * j : n * j + n] = s_ref[n * j :, n * j : n * j + n] - dot_nt(
                    low[o:], low[o : o + n]
                )
    put_x = pltpu.make_async_copy(x_ref, x_hbm, sem.at[0])
    put_x.start()
    put_x.wait()


def panel_kernel(
    ids_ref, x_hbm, y_hbm, p0, p1, p2, p3, factor_hbm, z_ref, x_ref, raw_ref, factor_ref, p_ref, y_ref, w_ref, sem
):
    n = TB
    my_row, core = ids_ref[0], lax.rem(ids_ref[1], 2)
    x, group = lax.rem(my_row, 4), lax.rem(ids_ref[1], 4)
    gets = [pltpu.make_async_copy(x_hbm, x_ref, sem.at[0]), pltpu.make_async_copy(y_hbm, raw_ref, sem.at[1])]
    for k, src in enumerate((p0, p1, p2, p3)):
        cols = pl.ds(pl.multiple_of((group ^ k) * n, n), n)
        gets.append(pltpu.make_async_copy(src, p_ref.at[:, cols], sem.at[2 + k]))
    for get in gets:
        get.start()
    gets[1].wait()
    for at, k in enumerate(ORDER):
        for c in range(16):
            y_ref[pl.ds(pl.multiple_of((x ^ k) * n + 8 * c, 8), 8), :] = raw_ref[c, 8 * at : 8 * at + 8, :]
    gets[0].wait()
    for i in range(0, LEAD, 2 * n):
        sl, upto = slice(i, i + 2 * n), i + 2 * n
        w_ref[sl, :] = dot(x_ref[sl, 0:upto], y_ref[0:upto, :])
    for get in gets[2:]:
        get.wait()
    for i in range(0, LEAD, 2 * n):
        sl, upto = slice(i, i + 2 * n), i + 2 * n
        inv = x_ref[sl, 0:upto]
        factor_ref[:, sl] = dot_nt(p_ref[:, 0:upto], inv)

    @pl.when(my_row < TILES)
    def _():
        row = lax.broadcasted_iota(jnp.int32, (n, LEAD), 0) + my_row * n
        lower = lax.broadcasted_iota(jnp.int32, (n, LEAD), 1) <= row
        factor_ref[0:n, :] = jnp.where(lower, factor_ref[0:n, :], 0.0)

    put = pltpu.make_async_copy(factor_ref, factor_hbm, sem.at[6])
    put.start()
    z = dot(factor_ref[pl.ds(pl.multiple_of(core * 256, 256), 256), :], w_ref[...])
    for a in range(2):
        for c in range(16):
            z_ref[16 * c + 8 * a : 16 * c + 8 * a + 8, :] = z[n * a + 8 * c : n * a + 8 * c + 8]

    @pl.when((my_row < TILES) & (core == 0))
    def _():
        for c in range(16):
            at = pl.multiple_of(my_row * n + 8 * c, 8)
            z_ref[16 * c : 16 * c + 8, :] = w_ref[pl.ds(at, 8), :]
    put.wait()


def trailing_kernel(
    ids_ref, x_hbm, factor_hbm, kernel_hbm, v_hbm, out_hbm,
    x_ref, factor_ref, kernel_ref, raw_ref, v_ref, high_ref, low_ref, out_ref, sem,
):
    n = TB
    my_row, my_col = ids_ref[0], ids_ref[1]
    gets = [pltpu.make_async_copy(v_hbm.at[k], raw_ref.at[k], sem.at[k]) for k in range(4)]
    get_x = pltpu.make_async_copy(x_hbm, x_ref, sem.at[4])
    get_factor = pltpu.make_async_copy(factor_hbm, factor_ref, sem.at[5])
    tiles = [pl.ds(8 * n * a, 8 * n) for a in range(4)]
    get_tiles = [
        pltpu.make_async_copy(kernel_hbm.at[at], kernel_ref.at[at], sem.at[6 + a])
        for a, at in enumerate(tiles)
    ]
    puts = [
        pltpu.make_async_copy(out_ref.at[at], out_hbm.at[at], sem.at[10 + a])
        for a, at in enumerate(tiles)
    ]
    for copy in [*gets, get_x, get_factor, *get_tiles]:
        copy.start()
    for k in range(4):
        gets[k].wait()
        for b in range(8):
            v_ref[n * k : n * k + n, n * b : n * b + n] = raw_ref[k, pl.ds(b, n, stride=8), :]
    get_x.wait()
    for i in range(0, LEAD, 2 * n):
        upto = i + 2 * n
        high, low = halves(dot(x_ref[i:upto, 0:upto], v_ref[0:upto, :]))
        high_ref[i:upto, :] = high
        low_ref[i:upto, :] = low
    get_factor.wait()
    for pair in range(2):
        get_tiles[2 * pair].wait()
        get_tiles[2 * pair + 1].wait()
        high, low = halves(factor_ref[2 * n * pair : 2 * n * pair + 2 * n, :])
        for h in range(4):
            cols = slice(256 * h, 256 * h + 256)
            update = dot_half(high, high_ref[:, cols]) + dot_half(high, low_ref[:, cols])
            update = update + dot_half(low, high_ref[:, cols])
            for up, half in ((0, 0), (0, 1), (1, 0), (1, 1)):
                a, b = 2 * pair + up, 2 * h + half
                at = pl.ds(8 * n * a + b, n, stride=8)
                left = kernel_ref[at, :] - update[n * up : n * up + n, n * half : n * half + n]
                if a == 0:
                    left = jnp.where(my_row < TILES, 0.0, left)
                if b == 0:
                    left = jnp.where(my_col < TILES, 0.0, left)
                out_ref[at, :] = left
        puts[2 * pair].start()
        puts[2 * pair + 1].start()
    for put in puts:
        put.wait()


def permute_z(block, hops):
    return lax.ppermute(block, "row", [(4 * a + x, 4 * b + x) for a, b in hops for x in range(4)])


def permute_xor(block, axis, k):
    return lax.ppermute(block, axis, [(i, i ^ k) for i in range(lax.axis_size(axis))])


def tree(block, depth, first):
    up, down = ([(0, 3)], [(0, 5)]) if first else ([(0, 1), (3, 4), (5, 6)], [(0, 7), (3, 2)])

    def pick(got):
        picked = block
        for hops, new in zip((up, down), got):
            hit = jnp.any(jnp.stack([depth == b for _, b in hops]))
            picked = jnp.where(hit, new, picked)
        return picked

    return [permute_z(block, up), permute_z(block, down)], pick


def per_device(kernel, targets):
    my_row = lax.axis_index("row")
    my_col = lax.axis_index("col")
    depth = my_row // 4
    f32 = jnp.float32
    ids = jnp.stack([my_row, my_col]).astype(jnp.int32)
    force = lax.optimization_barrier

    tile = kernel[0, :, 0, :]
    got = [lax.ppermute(tile, "col", [(c, c + d) for c in range(4)]) for d in (4, 8, 12)]
    tile = jnp.where(my_col < 4, tile, got[0] + got[1] + got[2])
    block = jnp.concatenate([tile, targets[0, 0].reshape(64, TB)], axis=0)
    got, pick = tree(block, depth, True)
    own = kernel[:, :, 0, :].reshape(LEAD, TB)
    block = pick(got)
    got, pick = tree(block, depth, False)
    own_got = lax.ppermute(own, "col", [(c, c + 8) for c in range(4)])
    got, own_got = force((got, own_got))
    block = pick(got)
    own = jnp.where((my_col >= 8) & (my_col < 12), own_got, own)

    block_1 = permute_xor(block, "row", 1)
    block_32 = permute_xor(jnp.concatenate([block, block_1], axis=0), "row", 3)
    lead = kernel[0].reshape(8 * TB, TB)
    got, pick = tree(lead, depth, True)
    own_got = lax.ppermute(own, "col", [(c, c + 4) for c in (0, 1, 2, 3, 8, 9, 10, 11)])
    block_32, got, own_got = force((block_32, got, own_got))
    lead = pick(got)
    own = jnp.where(my_col % 8 >= 4, own_got, own)
    blocks = [block, block_1, block_32[:192], block_32[192:]]

    t0 = jnp.concatenate([b[:TB] for b in blocks], axis=0)
    t2, t1 = permute_xor(t0, "col", 2), permute_xor(t0, "col", 1)
    got, pick = tree(lead, depth, False)
    wide = jnp.stack([b[TB:].reshape(8, 8, TB) for b in blocks]).transpose(2, 0, 1, 3)
    wide = lax.all_to_all(jnp.repeat(wide.reshape(8, 32, TB), 2, axis=0), "col", 0, 0)
    t3 = permute_xor(t2, "col", 1)
    t1, t3, got, wide = force((t1, t3, got, wide))
    panel = [own] + [permute_xor(own, "col", k) for k in (1, 2, 3)]
    leads = jnp.broadcast_to(pick(got)[None], (4, 8 * TB, TB))
    groups = [[4 * z + x for x in range(4)] for z in range(lax.axis_size("row") // 4)]
    leads = lax.all_to_all(leads, "row", 0, 0, axis_index_groups=groups)

    inverse = pl.pallas_call(
        chol_kernel,
        out_shape=jax.ShapeDtypeStruct((LEAD, LEAD), f32),
        in_specs=[SMEM] + [VMEM] * 4,
        out_specs=HBM,
        scratch_shapes=[
            pltpu.VMEM((LEAD, LEAD), f32),
            pltpu.VMEM((LEAD, LEAD), f32),
            pltpu.VMEM((TB, 2 * TB), f32),
            pltpu.SemaphoreType.DMA((1,)),
        ],
        compiler_params=pltpu.CompilerParams(vmem_limit_bytes=BIG),
        cost_estimate=pl.CostEstimate(flops=2 * 10**10, bytes_accessed=3 << 20, transcendentals=0),
    )(ids, t0, t1, t2, t3)
    inverse, leads = force((inverse, leads))

    factor, z = pl.pallas_call(
        panel_kernel,
        out_shape=[
            jax.ShapeDtypeStruct((LEAD, LEAD), f32),
            jax.ShapeDtypeStruct((2 * TB, TB), f32),
        ],
        in_specs=[SMEM] + [HBM] * 6,
        out_specs=[HBM, VMEM],
        scratch_shapes=[
            pltpu.VMEM((LEAD, LEAD), f32),
            pltpu.VMEM((16, 32, TB), f32),
            pltpu.VMEM((LEAD, LEAD), f32),
            pltpu.VMEM((LEAD, LEAD), f32),
            pltpu.VMEM((LEAD, TB), f32),
            pltpu.VMEM((LEAD, TB), f32),
            pltpu.SemaphoreType.DMA((7,)),
        ],
        compiler_params=pltpu.CompilerParams(vmem_limit_bytes=BIG),
        cost_estimate=pl.CostEstimate(flops=2 * 10**9, bytes_accessed=4 << 20, transcendentals=0),
    )(ids, inverse, wide, *panel)

    trailing = pl.pallas_call(
        trailing_kernel,
        out_shape=jax.ShapeDtypeStruct((8 * LEAD, TB), f32),
        in_specs=[SMEM] + [HBM] * 4,
        out_specs=HBM,
        scratch_shapes=[
            pltpu.VMEM((LEAD, LEAD), f32),
            pltpu.VMEM((LEAD, LEAD), f32),
            pltpu.VMEM((8 * LEAD, TB), f32),
            pltpu.VMEM((4, 8 * TB, TB), f32),
            pltpu.VMEM((LEAD, 8 * TB), f32),
            pltpu.VMEM((LEAD, 8 * TB), jnp.bfloat16),
            pltpu.VMEM((LEAD, 8 * TB), jnp.bfloat16),
            pltpu.VMEM((8 * LEAD, TB), f32),
            pltpu.SemaphoreType.DMA((14,)),
        ],
        compiler_params=pltpu.CompilerParams(vmem_limit_bytes=BIG),
        cost_estimate=pl.CostEstimate(flops=10**10, bytes_accessed=10 << 20, transcendentals=0),
    )(ids, inverse, factor, kernel.reshape(8 * LEAD, TB), leads)

    got = lax.all_to_all(z.reshape(16, 2, 8, TB), "col", 0, 0).reshape(8, 2, 2, 8, TB)
    got = got.transpose(1, 2, 3, 0, 4).reshape(4, 8, 8 * TB)
    top = (jnp.arange(4, dtype=jnp.int32) == 0)[:, None, None] & (my_row < TILES)
    targets_out = jnp.where(top, got, targets[:, 0] - got)[:, None]
    return (
        factor.reshape(4, TB, LEAD),
        trailing.reshape(kernel.shape),
        targets_out,
    )


def solution(mesh):
    return jax.shard_map(
        per_device,
        mesh=mesh,
        in_specs=(P(None, "row", None, "col"), P(None, "row", "col", None)),
        out_specs=(P(None, "row", None), P(None, "row", None, "col"), P(None, "row", "col", None)),
        check_vma=False,
    )
```

```python
import functools

import jax
import jax.numpy as jnp
from jax import lax
from jax.experimental import pallas as pl
from jax.experimental.pallas import tpu as pltpu
from jax.sharding import PartitionSpec as P

highest = lax.Precision.HIGHEST
TB = 128
LEAD = 512
TILES = LEAD // TB
ORDER = (0, 1, 3, 2)
BIG = 56 << 20
VMEM = pl.BlockSpec(memory_space=pltpu.VMEM)
HBM = pl.BlockSpec(memory_space=pltpu.HBM)
SMEM = pl.BlockSpec(memory_space=pltpu.SMEM)


def dot(a, b):
    return jnp.dot(a, b, precision=highest, preferred_element_type=jnp.float32)


def dot_nt(a, b):
    return lax.dot_general(
        a, b, (((1,), (1,)), ((), ())), precision=highest, preferred_element_type=jnp.float32
    )


def halves(a):
    high = a.astype(jnp.bfloat16)
    return high, (a - high.astype(jnp.float32)).astype(jnp.bfloat16)


def dot_half(a, b):
    return jnp.dot(a, b, preferred_element_type=jnp.float32)


def recip(p):
    r = pltpu.reciprocal(p, approx=True)
    return r * (2.0 - p * r)


def factor_tile(m_ref):
    n, w = TB, 8
    for g in range(n // w):
        base = w * g
        rows = [jnp.broadcast_to(m_ref[base + k : base + k + 1, 0:n], (8, n)) for k in range(w)]
        erow = [jnp.broadcast_to(m_ref[base + k : base + k + 1, n:], (8, n)) for k in range(w)]
        a, l, r = {}, {}, {}
        for k in range(w):
            for i in range(k + 1):
                a[k, i] = jnp.broadcast_to(rows[k][:, base + i : base + i + 1], (8, n))
        for i in range(w):
            r[i] = recip(a[i, i])
            for k in range(i + 1, w):
                l[k, i] = a[k, i] * r[i]
            for k in range(i + 1, w):
                for j in range(i + 1, k + 1):
                    a[k, j] = a[k, j] - l[k, i] * a[j, i]
                rows[k] = rows[k] - l[k, i] * rows[i]
                erow[k] = erow[k] - l[k, i] * erow[i]
        for k in range(w):
            m_ref[base + k : base + k + 1, n:] = (erow[k] * lax.rsqrt(a[k, k]))[0:1]
        if g == n // w - 1:
            break
        q = [rows[k] * r[k] for k in range(w)]
        qe = [erow[k] * r[k] for k in range(w)]
        for k in range(w - 1, -1, -1):
            for m in range(k + 1, w):
                q[k] = q[k] - l[m, k] * q[m]
                qe[k] = qe[k] - l[m, k] * qe[m]
        for rb in range(g + 1, n // w):
            d = m_ref[8 * rb : 8 * rb + 8, 0:n]
            e = m_ref[8 * rb : 8 * rb + 8, n:]
            cols = [jnp.broadcast_to(d[:, base + k : base + k + 1], (8, n)) for k in range(w)]
            for k in range(w):
                d = d - cols[k] * q[k]
                e = e - cols[k] * qe[k]
            m_ref[8 * rb : 8 * rb + 8, 0:n] = d
            m_ref[8 * rb : 8 * rb + 8, n:] = e


def chol_kernel(ids_ref, t0, t1, t2, t3, x_hbm, x_ref, s_ref, m_ref, sem):
    n = TB
    x, group = lax.rem(ids_ref[0], 4), lax.rem(ids_ref[1], 4)
    for m, src in enumerate((t0, t1, t2, t3)):
        for at, k in enumerate(ORDER):
            rows = pl.ds(pl.multiple_of((x ^ k) * n, n), n)
            cols = pl.ds(pl.multiple_of((group ^ m) * n, n), n)
            s_ref[rows, cols] = src[n * at : n * at + n, :]
    eye = (
        lax.broadcasted_iota(jnp.int32, (n, n), 0) == lax.broadcasted_iota(jnp.int32, (n, n), 1)
    ).astype(jnp.float32)
    for k in range(TILES):
        sl = slice(n * k, n * k + n)
        m_ref[:, 0:n] = s_ref[sl, sl]
        m_ref[:, n:] = eye
        factor_tile(m_ref)
        inv = m_ref[:, n:]
        if k > 0:
            x_ref[sl, 0 : n * k] = -dot(inv, dot(s_ref[sl, 0 : n * k], x_ref[0 : n * k, 0 : n * k]))
        x_ref[sl, sl] = inv
        if k < TILES - 1:
            x_ref[sl, n * (k + 1) :] = jnp.zeros((n, LEAD - n * (k + 1)), jnp.float32)
            low = dot_nt(s_ref[n * (k + 1) :, sl], inv)
            s_ref[n * (k + 1) :, sl] = low
            for j in range(k + 1, TILES):
                o = n * (j - k - 1)
                s_ref[n * j :, n * j : n * j + n] = s_ref[n * j :, n * j : n * j + n] - dot_nt(
                    low[o:], low[o : o + n]
                )
    put_x = pltpu.make_async_copy(x_ref, x_hbm, sem.at[0])
    put_x.start()
    put_x.wait()


def panel_kernel(
    ids_ref, x_hbm, y_hbm, p0, p1, p2, p3, factor_hbm, z_ref, x_ref, raw_ref, factor_ref, p_ref, y_ref, w_ref, sem
):
    n = TB
    my_row, core = ids_ref[0], lax.rem(ids_ref[1], 2)
    x, group = lax.rem(my_row, 4), lax.rem(ids_ref[1], 4)
    gets = [pltpu.make_async_copy(x_hbm, x_ref, sem.at[0]), pltpu.make_async_copy(y_hbm, raw_ref, sem.at[1])]
    for k, src in enumerate((p0, p1.at[LEAD:], p2, p3)):
        cols = pl.ds(pl.multiple_of((group ^ k) * n, n), n)
        gets.append(pltpu.make_async_copy(src, p_ref.at[:, cols], sem.at[2 + k]))
    for get in gets:
        get.start()
    gets[1].wait()
    for at, k in enumerate(ORDER):
        for c in range(16):
            y_ref[pl.ds(pl.multiple_of((x ^ k) * n + 8 * c, 8), 8), :] = raw_ref[c, 8 * at : 8 * at + 8, :]
    gets[0].wait()
    for i in range(0, LEAD, 2 * n):
        sl, upto = slice(i, i + 2 * n), i + 2 * n
        w_ref[sl, :] = dot(x_ref[sl, 0:upto], y_ref[0:upto, :])
    for get in gets[2:]:
        get.wait()
    for i in range(0, LEAD, 2 * n):
        sl, upto = slice(i, i + 2 * n), i + 2 * n
        inv = x_ref[sl, 0:upto]
        factor_ref[:, sl] = dot_nt(p_ref[:, 0:upto], inv)

    @pl.when(my_row < TILES)
    def _():
        row = lax.broadcasted_iota(jnp.int32, (n, LEAD), 0) + my_row * n
        lower = lax.broadcasted_iota(jnp.int32, (n, LEAD), 1) <= row
        factor_ref[0:n, :] = jnp.where(lower, factor_ref[0:n, :], 0.0)

    put = pltpu.make_async_copy(factor_ref, factor_hbm, sem.at[6])
    put.start()
    z = dot(factor_ref[pl.ds(pl.multiple_of(core * 256, 256), 256), :], w_ref[...])
    for a in range(2):
        for c in range(16):
            z_ref[16 * c + 8 * a : 16 * c + 8 * a + 8, :] = z[n * a + 8 * c : n * a + 8 * c + 8]

    @pl.when((my_row < TILES) & (core == 0))
    def _():
        for c in range(16):
            at = pl.multiple_of(my_row * n + 8 * c, 8)
            z_ref[16 * c : 16 * c + 8, :] = w_ref[pl.ds(at, 8), :]
    put.wait()


def trailing_kernel(
    ids_ref, x_hbm, factor_hbm, kernel_hbm, v_hbm, out_hbm,
    x_ref, factor_ref, kernel_ref, raw_ref, v_ref, high_ref, low_ref, out_ref, sem,
):
    n = TB
    my_row, my_col = ids_ref[0], ids_ref[1]
    gets = [pltpu.make_async_copy(v_hbm.at[k], raw_ref.at[k], sem.at[k]) for k in range(4)]
    get_x = pltpu.make_async_copy(x_hbm, x_ref, sem.at[4])
    get_factor = pltpu.make_async_copy(factor_hbm, factor_ref, sem.at[5])
    tiles = [pl.ds(8 * n * a, 8 * n) for a in range(4)]
    get_tiles = [
        pltpu.make_async_copy(kernel_hbm.at[at], kernel_ref.at[at], sem.at[6 + a])
        for a, at in enumerate(tiles)
    ]
    puts = [
        pltpu.make_async_copy(out_ref.at[at], out_hbm.at[at], sem.at[10 + a])
        for a, at in enumerate(tiles)
    ]
    for copy in [*gets, get_x, get_factor, *get_tiles]:
        copy.start()
    for k in range(4):
        gets[k].wait()
        for b in range(8):
            v_ref[n * k : n * k + n, n * b : n * b + n] = raw_ref[k, pl.ds(b, n, stride=8), :]
    get_x.wait()
    for i in range(0, LEAD, 2 * n):
        upto = i + 2 * n
        high, low = halves(dot(x_ref[i:upto, 0:upto], v_ref[0:upto, :]))
        high_ref[i:upto, :] = high
        low_ref[i:upto, :] = low
    get_factor.wait()
    for pair in range(2):
        get_tiles[2 * pair].wait()
        get_tiles[2 * pair + 1].wait()
        high, low = halves(factor_ref[2 * n * pair : 2 * n * pair + 2 * n, :])
        for h in range(4):
            cols = slice(256 * h, 256 * h + 256)
            update = dot_half(high, high_ref[:, cols]) + dot_half(high, low_ref[:, cols])
            update = update + dot_half(low, high_ref[:, cols])
            for up, half in ((0, 0), (0, 1), (1, 0), (1, 1)):
                a, b = 2 * pair + up, 2 * h + half
                at = pl.ds(8 * n * a + b, n, stride=8)
                left = kernel_ref[at, :] - update[n * up : n * up + n, n * half : n * half + n]
                if a == 0:
                    left = jnp.where(my_row < TILES, 0.0, left)
                if b == 0:
                    left = jnp.where(my_col < TILES, 0.0, left)
                out_ref[at, :] = left
        puts[2 * pair].start()
        puts[2 * pair + 1].start()
    for put in puts:
        put.wait()


def permute_z(block, hops):
    return lax.ppermute(block, "row", [(4 * a + x, 4 * b + x) for a, b in hops for x in range(4)])


def permute_xor(block, axis, k):
    return lax.ppermute(block, axis, [(i, i ^ k) for i in range(lax.axis_size(axis))])


def tree(block, depth, first):
    up, down = ([(0, 3)], [(0, 5)]) if first else ([(0, 1), (3, 4), (5, 6)], [(0, 7), (3, 2)])

    def pick(got):
        picked = block
        for hops, new in zip((up, down), got):
            hit = jnp.any(jnp.stack([depth == b for _, b in hops]))
            picked = jnp.where(hit, new, picked)
        return picked

    return [permute_z(block, up), permute_z(block, down)], pick


def per_device(kernel, targets):
    my_row = lax.axis_index("row")
    my_col = lax.axis_index("col")
    depth = my_row // 4
    f32 = jnp.float32
    ids = jnp.stack([my_row, my_col]).astype(jnp.int32)
    force = lax.optimization_barrier

    tile = kernel[0, :, 0, :]
    got = [lax.ppermute(tile, "col", [(c, c + d) for c in range(4)]) for d in (4, 8, 12)]
    tile = jnp.where(my_col < 4, tile, got[0] + got[1] + got[2])
    block = jnp.concatenate([tile, targets[0, 0].reshape(64, TB)], axis=0)
    got, pick = tree(block, depth, True)
    own = kernel[:, :, 0, :].reshape(LEAD, TB)
    block = pick(got)
    got, pick = tree(block, depth, False)
    own_got = lax.ppermute(own, "col", [(c, c + 8) for c in range(4)])
    got, own_got = force((got, own_got))
    block = pick(got)
    own = jnp.where((my_col >= 8) & (my_col < 12), own_got, own)

    block_1 = permute_xor(block, "row", 1)
    block_32 = permute_xor(jnp.concatenate([block, block_1], axis=0), "row", 3)
    lead = kernel[0].reshape(8 * TB, TB)
    got, pick = tree(lead, depth, True)
    own_got = lax.ppermute(own, "col", [(c, c + 4) for c in (0, 1, 2, 3, 8, 9, 10, 11)])
    block_32, got, own_got = force((block_32, got, own_got))
    lead = pick(got)
    own = jnp.where(my_col % 8 >= 4, own_got, own)
    blocks = [block, block_1, block_32[:192], block_32[192:]]

    t0 = jnp.concatenate([b[:TB] for b in blocks], axis=0)
    t2 = permute_xor(t0, "col", 2)
    t1 = permute_xor(jnp.concatenate([t0, own], axis=0), "col", 1)
    got, pick = tree(lead, depth, False)
    wide = jnp.stack([b[TB:].reshape(8, 8, TB) for b in blocks]).transpose(2, 0, 1, 3)
    wide = lax.all_to_all(jnp.repeat(wide.reshape(8, 32, TB), 2, axis=0), "col", 0, 0)
    t3 = permute_xor(t2, "col", 1)
    t1, t3, got, wide = force((t1, t3, got, wide))
    panel = [own, t1, permute_xor(own, "col", 2), permute_xor(own, "col", 3)]
    leads = jnp.broadcast_to(pick(got)[None], (4, 8 * TB, TB))
    groups = [[4 * z + x for x in range(4)] for z in range(lax.axis_size("row") // 4)]
    leads = lax.all_to_all(leads, "row", 0, 0, axis_index_groups=groups)

    inverse = pl.pallas_call(
        chol_kernel,
        out_shape=jax.ShapeDtypeStruct((LEAD, LEAD), f32),
        in_specs=[SMEM] + [VMEM] * 4,
        out_specs=HBM,
        scratch_shapes=[
            pltpu.VMEM((LEAD, LEAD), f32),
            pltpu.VMEM((LEAD, LEAD), f32),
            pltpu.VMEM((TB, 2 * TB), f32),
            pltpu.SemaphoreType.DMA((1,)),
        ],
        compiler_params=pltpu.CompilerParams(vmem_limit_bytes=BIG),
        cost_estimate=pl.CostEstimate(flops=2 * 10**10, bytes_accessed=3 << 20, transcendentals=0),
    )(ids, t0, t1, t2, t3)
    inverse, leads = force((inverse, leads))

    factor, z = pl.pallas_call(
        panel_kernel,
        out_shape=[
            jax.ShapeDtypeStruct((LEAD, LEAD), f32),
            jax.ShapeDtypeStruct((2 * TB, TB), f32),
        ],
        in_specs=[SMEM] + [HBM] * 6,
        out_specs=[HBM, VMEM],
        scratch_shapes=[
            pltpu.VMEM((LEAD, LEAD), f32),
            pltpu.VMEM((16, 32, TB), f32),
            pltpu.VMEM((LEAD, LEAD), f32),
            pltpu.VMEM((LEAD, LEAD), f32),
            pltpu.VMEM((LEAD, TB), f32),
            pltpu.VMEM((LEAD, TB), f32),
            pltpu.SemaphoreType.DMA((7,)),
        ],
        compiler_params=pltpu.CompilerParams(vmem_limit_bytes=BIG),
        cost_estimate=pl.CostEstimate(flops=2 * 10**9, bytes_accessed=4 << 20, transcendentals=0),
    )(ids, inverse, wide, *panel)

    trailing = pl.pallas_call(
        trailing_kernel,
        out_shape=jax.ShapeDtypeStruct((8 * LEAD, TB), f32),
        in_specs=[SMEM] + [HBM] * 4,
        out_specs=HBM,
        scratch_shapes=[
            pltpu.VMEM((LEAD, LEAD), f32),
            pltpu.VMEM((LEAD, LEAD), f32),
            pltpu.VMEM((8 * LEAD, TB), f32),
            pltpu.VMEM((4, 8 * TB, TB), f32),
            pltpu.VMEM((LEAD, 8 * TB), f32),
            pltpu.VMEM((LEAD, 8 * TB), jnp.bfloat16),
            pltpu.VMEM((LEAD, 8 * TB), jnp.bfloat16),
            pltpu.VMEM((8 * LEAD, TB), f32),
            pltpu.SemaphoreType.DMA((14,)),
        ],
        compiler_params=pltpu.CompilerParams(vmem_limit_bytes=BIG),
        cost_estimate=pl.CostEstimate(flops=10**10, bytes_accessed=10 << 20, transcendentals=0),
    )(ids, inverse, factor, kernel.reshape(8 * LEAD, TB), leads)

    got = lax.all_to_all(z.reshape(16, 2, 8, TB), "col", 0, 0).reshape(8, 2, 2, 8, TB)
    got = got.transpose(1, 2, 3, 0, 4).reshape(4, 8, 8 * TB)
    top = (jnp.arange(4, dtype=jnp.int32) == 0)[:, None, None] & (my_row < TILES)
    targets_out = jnp.where(top, got, targets[:, 0] - got)[:, None]
    return (
        factor.reshape(4, TB, LEAD),
        trailing.reshape(kernel.shape),
        targets_out,
    )


def solution(mesh):
    return jax.shard_map(
        per_device,
        mesh=mesh,
        in_specs=(P(None, "row", None, "col"), P(None, "row", "col", None)),
        out_specs=(P(None, "row", None), P(None, "row", None, "col"), P(None, "row", "col", None)),
        check_vma=False,
    )
```
